128 devices in a mesh: dp: 16 (over z_hi, y, core), ctx: 8 (over z_lo, x).
Axes of the slice: x: 4, y: 4, z: 4 (z_hi: 2, z_lo: 2; z = z_hi * 2 + z_lo), core: 2. Of those that a mesh axis runs over, the one named last changes fastest.
Arguments:
- token_ids: int32 [16, 1024], P('dp', 'ctx'), may hold values from 0 to 511
- bucket_of_slot: int32 [32], replicated, may hold values from 0 to 31, each once
- embed_tiles: bfloat16 [32, 512, 128], P('dp'), may hold values from -6 to 6
- norm_gain: float32 [4096], replicated, may hold values from 0.1 to 1.9
- in_tiles: bfloat16 [32, 128, 3, 4096], P('dp', None, None, 'ctx'), may hold values from -0.09375 to 0.09375
- short_taps: float32 [3, 3, 4096], P(None, None, 'ctx'), may hold values from -3 to 3
- decay_rate: float32 [16, 256], P(None, 'ctx'), may hold values from 0.002 to 0.05
- residue: float32 [16, 256], P(None, 'ctx'), may hold values from -0.3 to 0.3
- skip_gain: float32 [4096], P('ctx'), may hold values from -4 to 4
- out_tiles: bfloat16 [32, 128, 4096], P('dp', None, 'ctx'), may hold values from -0.09375 to 0.09375
Outputs:
- hidden_out: bfloat16 [16, 1024, 4096], P('dp', 'ctx')
The draws below stay inside these ranges and needn't reach their ends.
Inputs may be any that keep to these rules, and one draw needn't show every extreme that they name: `bucket_of_slot`: each bucket stands in exactly one slot; slot s is kept by dp index s // 2.
All inputs are finite; a program needn't handle non-finite values.
Results may differ from the reference program's by a relative error of at most 0.02.
Values may be sent and summed in bfloat16 or wider, within the bound.
No kernel may reach another device: no remote copies, remote signals or barrier semaphores. Data moves between devices by JAX's collectives and lax.ppermute only.
A program may use at most 192 MiB of HBM per device.

```python
import math
import jax
import jax.numpy as jnp
import numpy as np
from jax import lax

D = 4096
HC = 4096
VOCAB = 512
MODES = 16
GSIZE = 16
SEQ = 1024
BUCKETS = 32
CHAN_DEV = 512
GROUPS = 256
N_DP = 16
N_CTX = 8


def place_ends(result, own_key, low, high):
    spot = [jax.random.randint(jax.random.fold_in(own_key, axis), (), 0, length) for axis, length in enumerate(result.shape)]
    longest = result.shape.index(max(result.shape))
    next_to = spot[:longest] + [(spot[longest] + 1) % result.shape[longest]] + spot[longest + 1:]
    return result.at[tuple(spot)].set(low).at[tuple(next_to)].set(high)


def block_levels(own_key, extent, shards, low, top_value):
    factor_of = 1.0
    for dim, shards_of in shards:
        steps = jax.random.uniform(jax.random.fold_in(jax.random.fold_in(own_key, 6), dim), (shards_of,), jnp.float32, low / len(shards), top_value / len(shards))
        factor_of = factor_of * jnp.repeat(jnp.exp(steps), extent[dim] // shards_of).reshape((-1,) + (1,) * (len(extent) - 1 - dim))
    return factor_of


def cumulative_ranks(number_of, skew):
    portions = [(1 << 20) // math.isqrt(standing ** skew) + 1 for standing in range(1, number_of + 1)]
    spread = 1 + sum(portions) // (1 << 30)
    return np.cumsum(np.array([max(1, weight // spread) for weight in portions]))


def skewed_ids(stream_key, dims, number_of, slope):
    table = cumulative_ranks(number_of, slope)
    pick = jax.random.randint(jax.random.fold_in(stream_key, 1), dims, 0, int(table[number_of - 1]))
    grade = jnp.searchsorted(jnp.asarray(table, jnp.int32), pick, side="right")
    return jax.random.permutation(jax.random.fold_in(stream_key, 2), number_of)[grade].astype(jnp.int32)


def gaussian(stream_key, dims, width, most, split=(), held_as=jnp.bfloat16):
    factor_of = block_levels(stream_key, dims, split, -0.22, 0.18) if split else 1.0
    entries = jax.random.normal(stream_key, dims, jnp.float32) * width * factor_of
    return jnp.minimum(jnp.maximum(entries, -most), most).astype(held_as)


def setup_inputs(seed: int = 0) -> dict:
    streams_of = jax.random.split(jax.random.key(seed), 11)
    token_ids = place_ends(skewed_ids(streams_of[0], (N_DP, SEQ), VOCAB, 2), jax.random.fold_in(streams_of[0], 3), 0, VOCAB - 1).astype(jnp.int32)
    bucket_of_slot = jax.random.permutation(streams_of[1], BUCKETS).astype(jnp.int32)
    embed_tiles = gaussian(streams_of[2], (BUCKETS, VOCAB, D // BUCKETS), 1.0, 6.0, ((0, 16),))
    norm_gain = jnp.clip(1.0 + 0.18 * jax.random.normal(streams_of[3], (D,), jnp.float32), 0.1, 1.9)
    in_tiles = gaussian(streams_of[4], (BUCKETS, D // BUCKETS, 3, HC), D ** -0.5, 0.09375, ((0, 16), (3, 8)))
    short_taps = gaussian(streams_of[5], (3, 3, HC), 0.6, 3.0, ((2, 8),), jnp.float32)
    decay_rate = jnp.clip(jnp.exp(math.log(0.05) - 3.218876 * jax.random.uniform(streams_of[6], (MODES, GROUPS), jnp.float32) ** block_levels(streams_of[6], (MODES, GROUPS), ((1, 8),), -0.2, 0.2)), 0.002, 0.05)
    residue = gaussian(streams_of[7], (MODES, GROUPS), 0.05, 0.3, ((1, 8),), jnp.float32)
    skip_gain = gaussian(streams_of[8], (HC,), 1.0, 4.0, ((0, 8),), jnp.float32)
    out_tiles = gaussian(streams_of[9], (BUCKETS, D // BUCKETS, HC), HC ** -0.5, 0.09375, ((0, 16), (2, 8)))
    return {"token_ids": token_ids, "bucket_of_slot": bucket_of_slot, "embed_tiles": embed_tiles, "norm_gain": norm_gain, "in_tiles": in_tiles, "short_taps": short_taps, "decay_rate": decay_rate, "residue": residue, "skip_gain": skip_gain, "out_tiles": out_tiles}


def bucket_order(bucket_of_slot):
    slot_index = jnp.arange(BUCKETS, dtype=jnp.int32)
    hits = (bucket_of_slot[:, None] == slot_index[None, :]).astype(jnp.int32)
    return lax.optimization_barrier(jnp.sum(slot_index[:, None] * hits, axis=0)).astype(jnp.int32)

def reference(token_ids, bucket_of_slot, embed_tiles, norm_gain, in_tiles, short_taps, decay_rate, residue, skip_gain, out_tiles):
    slot_of_bucket = bucket_order(bucket_of_slot)
    table = jnp.transpose(embed_tiles[slot_of_bucket], (1, 0, 2)).reshape(VOCAB, D)
    w_in = in_tiles[slot_of_bucket].reshape(D, 3 * HC)
    w_out = out_tiles[slot_of_bucket].reshape(D, HC)
    times = jnp.arange(SEQ).astype(jnp.float32)
    filter_taps = jnp.einsum('mg,mgt->tg', residue, jnp.exp(-decay_rate[:, :, None] * times[None, None, :]), precision=lax.Precision.HIGHEST)
    filter_taps = filter_taps.astype(jnp.bfloat16).astype(jnp.float32)
    filter_chan = jnp.repeat(filter_taps, GSIZE, axis=1)
    filter_hat = jnp.fft.rfft(filter_chan, n=2 * SEQ, axis=0)

    def one_sequence(sequence_ids):
        embedded = table[sequence_ids]
        embed_f32 = embedded.astype(jnp.float32)
        scale = lax.rsqrt(lax.optimization_barrier(jnp.mean(embed_f32 * embed_f32, axis=-1, keepdims=True)) + 1e-06)
        normed = (embed_f32 * scale * norm_gain).astype(jnp.bfloat16)
        projected = jnp.dot(normed, w_in, preferred_element_type=jnp.float32).reshape(SEQ, 3, HC)
        padded = jnp.pad(projected, ((2, 0), (0, 0), (0, 0)))
        featured = short_taps[0] * projected + short_taps[1] * padded[1:SEQ + 1] + short_taps[2] * padded[0:SEQ]
        query_part = featured[:, 0]
        product = (featured[:, 1] * featured[:, 2]).astype(jnp.bfloat16).astype(jnp.float32)
        spectrum = jnp.fft.rfft(product, n=2 * SEQ, axis=0) * filter_hat
        long_conv = jnp.fft.irfft(spectrum, n=2 * SEQ, axis=0)[:SEQ]
        mixed = long_conv + skip_gain * product
        gated = (query_part * mixed).astype(jnp.bfloat16)
        running = jnp.zeros((SEQ, D), jnp.float32)
        for group in range(N_CTX):
            first = group * CHAN_DEV
            share = jnp.dot(gated[:, first:first + CHAN_DEV], w_out[:, first:first + CHAN_DEV].T, preferred_element_type=jnp.float32)
            share = lax.optimization_barrier(share.astype(jnp.bfloat16))
            running = running + share.astype(jnp.float32)
        return (embed_f32 + running).astype(jnp.bfloat16)
    return lax.map(one_sequence, token_ids)
```

```python
import jax
import jax.numpy as jnp
from jax import lax
from jax.experimental import pallas as pl
from jax.experimental.pallas import tpu as pltpu
from jax.sharding import Mesh
from jax.sharding import PartitionSpec as P

F32 = jnp.float32
BF16 = jnp.bfloat16
D = 4096
SEQ = 1024
EPS = 1e-06
OFFSETS = (0, 3, 1, 2)
ZAX = ("zh", "zl")
DP = ("zh", "y", "co")
CTX = ("zl", "x")


def shift(value, axis, step):
    return lax.ppermute(value, axis, [(i, (i + step) % 4) for i in range(4)])


def flip(value, axes, bits, size):
    return lax.ppermute(value, axes, [(i, i ^ bits) for i in range(size)])


def ring(value, axis):
    half = value.shape[0] // 2
    below = shift(value, axis, 1)
    above = shift(value, axis, -1)
    first = shift(below[:half], axis, 1)
    second = shift(above[half:], axis, -1)
    return value, below, above, first, second


def gather_cube(part, order):
    for axis in order[:2]:
        part = jnp.concatenate(ring(part, axis))
    return ring(part, order[2])


def mixer_kernel(recv, taps, skip, decay, residue, out, toep, prod, query):
    table = recv[0, 0:96, :].astype(F32)
    extra = recv[0, 96:112, :].astype(F32)
    square = extra[8:9] + extra[9:10]
    for i in range(1, 8):
        table = table + recv[i, 0:96, :].astype(F32)
        extra = recv[i, 96:112, :].astype(F32)
        square = square + extra[8:9] + extra[9:10]
    table = (table * lax.rsqrt(square / D + EPS)).astype(BF16)

    for g in range(2):
        time = lax.broadcasted_iota(jnp.int32, (16, SEQ), 1).astype(F32)
        terms = jnp.exp(-decay[:, g : g + 1] * time) * residue[:, g : g + 1]
        filt = jnp.sum(terms, axis=0, keepdims=True).astype(BF16).astype(F32)
        filt = jnp.concatenate([filt, jnp.zeros((1, 128), F32)], axis=1)
        lagged = pltpu.roll(
            jnp.broadcast_to(filt, (128, SEQ + 128)), 0, 1, stride=1, stride_axis=0
        ).astype(BF16)
        for k in range(4):
            toep[g, k, 0:128, :] = lagged[:, 256 * k : 256 * k + 256]
            if k == 0:
                toep[g, k, 128:256, 0:128] = jnp.zeros((128, 128), BF16)
                toep[g, k, 128:256, 128:256] = lagged[:, 0:128]
            else:
                toep[g, k, 128:256, :] = lagged[:, 256 * k - 128 : 256 * k + 128]

    vocab = lax.broadcasted_iota(jnp.int32, (512, 512), 0).astype(F32)
    lane = lax.broadcasted_iota(jnp.int32, (96, SEQ), 1)

    def one_pair(i, carry):
        extra = recv[i, 96:112, :].astype(F32)
        for j in range(2):
            parts = []
            for a in range(2):
                r = 2 * j + a
                ids = extra[r : r + 1] * 256.0 + extra[4 + r : 5 + r]
                hot = jnp.where(vocab == ids, 1.0, 0.0).astype(BF16)
                parts.append(jnp.dot(table, hot, preferred_element_type=F32))
            z0 = jnp.concatenate(parts, axis=1)
            z1 = jnp.where(lane >= 1, pltpu.roll(z0, 1, 1), 0.0)
            z2 = jnp.where(lane >= 2, pltpu.roll(z0, 2, 1), 0.0)
            f = taps[0] * z0 + taps[1] * z1 + taps[2] * z2
            u = (f[32:64] * f[64:96]).astype(BF16)
            rows = pl.ds(pl.multiple_of((2 * i + j) * 16, 16), 16)
            for g in range(2):
                for b in range(4):
                    cols = slice(256 * b, 256 * b + 256)
                    prod[g, b, rows, :] = u[16 * g : 16 * g + 16, cols]
                    query[g, b, rows, :] = f[16 * g : 16 * g + 16, cols]
        return carry

    lax.fori_loop(0, 8, one_pair, 0)

    for g in range(2):
        for b in range(4):
            mixed = skip[g] * prod[g, b].astype(F32)
            for a in range(b + 1):
                mixed = mixed + jnp.dot(prod[g, a], toep[g, b - a], preferred_element_type=F32)
            gated = (query[g, b] * mixed).astype(BF16)
            for n in range(16):
                for h in range(2):
                    out[
                        2 * b + h,
                        n // 2,
                        16 * g : 16 * g + 16,
                        128 * (n % 2) : 128 * (n % 2) + 128,
                    ] = gated[16 * n : 16 * n + 16, 128 * h : 128 * h + 128]


def mixer(recv, taps, skip, decay, residue):
    vmem = pl.BlockSpec(memory_space=pltpu.VMEM)
    return pl.pallas_call(
        mixer_kernel,
        out_shape=jax.ShapeDtypeStruct((8, 8, 32, 256), BF16),
        in_specs=[vmem] * 5,
        out_specs=vmem,
        scratch_shapes=[
            pltpu.VMEM((2, 4, 256, 256), BF16),
            pltpu.VMEM((2, 4, 256, 256), BF16),
            pltpu.VMEM((2, 4, 256, 256), F32),
        ],
        compiler_params=pltpu.CompilerParams(vmem_limit_bytes=32 << 20),
        cost_estimate=pl.CostEstimate(
            flops=2 * 16 * 96 * 512 * 1024, bytes_accessed=4 << 20, transcendentals=0
        ),
        name="mixer",
    )(recv, taps, skip, decay, residue)


def project_kernel(where, bucket, gated, ids, *refs):
    pieces = [refs[5 * p : 5 * p + 5] for p in range(3)]
    own, other, total, embed = refs[15:]
    x, y, z, co = where[0], where[1], where[2], where[3]
    total[...] = jnp.zeros_like(total)

    def block(p, rel):
        near, mid, far = rel
        at = mid * 4 + near
        if far < 3:
            return pieces[p][far], 4 * at
        return (pieces[p][3], 4 * at) if at < 8 else (pieces[p][4], 4 * (at - 8))

    for yr in range(4):
        for zr in range(4):
            y_of = lax.rem(y + OFFSETS[yr], 4)
            z_of = lax.rem(z + OFFSETS[zr], 4)
            owner = (z_of // 2) * 4 + y_of
            left, right = [], []
            for xr in range(4):
                chunk = lax.rem(z_of, 2) * 4 + lax.rem(x + OFFSETS[xr], 4)
                rel = ((xr, yr, zr), (yr, zr, xr), (zr, xr, yr))
                rows = []
                for p in range(3):
                    ref, at = block(p, rel[p])
                    if p < 2:
                        rows.append(ref[at : at + 4].reshape(192, 256))
                    else:
                        rows.append(ref[at : at + 4, 0:32].reshape(128, 256))
                        for s in range(4):
                            for h in range(2):
                                at_row = pl.multiple_of(chunk * 32 + 16 * h, 16)
                                embed[owner, pl.ds(at_row, 16), 128 * s : 128 * s + 128] = ref[
                                    at + s, 32:48, 128 * h : 128 * h + 128
                                ]
                left.append(jnp.concatenate(rows, axis=0))
                right.append(gated[chunk])
            total[owner] += jnp.dot(
                jnp.concatenate(left, axis=1),
                jnp.concatenate(right, axis=0),
                preferred_element_type=F32,
            )

    lane = lax.broadcasted_iota(jnp.int32, (256, 256), 1)
    vocab = lane + (lane // 32) * 32 + co * 32
    hot = jnp.where(ids[...] == vocab, 1.0, 0.0).astype(BF16)
    for owner in range(8):
        looked = jnp.dot(hot, embed[owner], preferred_element_type=F32)
        for s in range(4):
            rows = jnp.concatenate(
                [
                    total[owner, 48 * s : 48 * s + 48],
                    total[owner, 192 + 48 * s : 240 + 48 * s],
                    total[owner, 384 + 32 * s : 416 + 32 * s],
                ],
                axis=0,
            )
            both = rows.T + looked[:, 128 * s : 128 * s + 128]
            core = co if s < 2 else 1 - co
            slot = 4 * owner + 2 * core + s % 2
            cols = pl.ds(pl.multiple_of(bucket[slot] * 128, 128), 128)
            own[:, cols] = jnp.where(co == 0, both[0:128], both[128:256])
            other[:, cols] = jnp.where(co == 0, both[128:256], both[0:128]).astype(BF16)


def project(where, bucket, gated, ids, pieces):
    vmem = pl.BlockSpec(memory_space=pltpu.VMEM)
    smem = pl.BlockSpec(memory_space=pltpu.SMEM)
    return pl.pallas_call(
        project_kernel,
        out_shape=(
            jax.ShapeDtypeStruct((128, D), F32),
            jax.ShapeDtypeStruct((128, D), BF16),
        ),
        in_specs=[smem, smem] + [vmem] * (2 + len(pieces)),
        out_specs=(vmem, vmem),
        scratch_shapes=[
            pltpu.VMEM((8, 512, 256), F32),
            pltpu.VMEM((8, 256, 512), BF16),
        ],
        compiler_params=pltpu.CompilerParams(vmem_limit_bytes=48 << 20),
        cost_estimate=pl.CostEstimate(
            flops=2 * 256 * 4096 * 2048, bytes_accessed=24 << 20, transcendentals=0
        ),
        name="project",
    )(where, bucket, gated, ids, *pieces)


def body(
    token_ids,
    bucket_of_slot,
    embed_tiles,
    norm_gain,
    in_tiles,
    short_taps,
    decay_rate,
    residue,
    skip_gain,
    out_tiles,
):
    zh, y, co, zl, x = (lax.axis_index(a) for a in ("zh", "y", "co", "zl", "x"))
    zy = zh * 4 + y
    c = zl * 4 + x
    d = zy * 2 + co

    def tile_for(core):
        rows = lax.dynamic_slice_in_dim(out_tiles, core * 256, 256, axis=2)
        words = lax.dynamic_slice_in_dim(embed_tiles, (c * 2 + core) * 32, 32, axis=1)
        words = words.reshape(2, 2, 16, 128).transpose(0, 2, 1, 3).reshape(2, 16, 256)
        return jnp.concatenate([rows, words], axis=1)

    tiles = jnp.concatenate([tile_for(co), flip(tile_for(1 - co), "co", 1, 2)])
    pieces = []
    for p, order in enumerate((("x", "y", ZAX), ("y", ZAX, "x"), (ZAX, "x", "y"))):
        pieces += gather_cube(tiles[:, 48 * p : 48 * p + 48], order)

    core_index = lax.broadcasted_iota(jnp.int32, (2, 8, 128), 0)
    ctx_index = lax.broadcasted_iota(jnp.int32, (2, 8, 128), 1)
    ids = jnp.where((core_index == co) & (ctx_index == c), token_ids[None], 0)
    ids = ids + shift(ids, "x", 1) + shift(ids, "x", -1) + shift(ids, "x", 2)
    ids = ids + sum(flip(ids, ("co", "zl"), b, 4) for b in (1, 2, 3))
    here = lax.dynamic_index_in_dim(ids, c, 1, keepdims=False).reshape(256, 1)
    ids = ids.reshape(4, 512)
    ids_rows = jnp.concatenate([ids // 256, ids % 256]).astype(BF16)

    buckets = lax.dynamic_slice_in_dim(bucket_of_slot, 2 * d, 2)
    gain = jnp.take(norm_gain.reshape(32, 128), buckets, axis=0)
    embed_f32 = embed_tiles.astype(F32)
    scaled = (embed_f32 * gain[:, None, :]).astype(BF16)
    square = jnp.sum(embed_f32 * embed_f32, axis=(0, 2))
    high = lax.reduce_precision(square, 8, 7)
    square_rows = jnp.stack([high, square - high]).astype(BF16)

    def partial_for(core):
        weights = lax.dynamic_slice_in_dim(in_tiles, core * 256, 256, axis=3)
        weights = weights.reshape(2, 128, 3, 8, 32).transpose(0, 1, 3, 2, 4).reshape(2, 128, 768)
        return lax.dot_general(
            weights, scaled, (((0, 1), (0, 2)), ((), ())), preferred_element_type=F32
        )

    given = jnp.concatenate(
        [partial_for(1 - co).astype(BF16), square_rows, jnp.zeros((14, 512), BF16)]
    )
    taken = flip(given, "co", 1, 2).astype(F32)
    table = (partial_for(co) + taken[:768]).astype(BF16).reshape(8, 96, 512)
    square = square + taken[768] + taken[769]
    high = lax.reduce_precision(square, 8, 7)
    square_rows = jnp.stack([high, square - high]).astype(BF16)
    extra = jnp.concatenate([ids_rows, square_rows, jnp.zeros((6, 512), BF16)])
    packed = jnp.concatenate([table, jnp.broadcast_to(extra[None], (8, 16, 512))], axis=1)
    packed = lax.all_to_all(packed, ("zh", "y"), split_axis=0, concat_axis=0, tiled=True)

    first = co * 256 + zy * 32
    taps = lax.dynamic_slice_in_dim(short_taps, first, 32, axis=2).reshape(3, 96, 1)
    skip = lax.dynamic_slice_in_dim(skip_gain, first, 32).reshape(2, 1, 16)
    skip = jnp.broadcast_to(skip, (2, 16, 16)).reshape(2, 256, 1)
    decay = lax.dynamic_slice_in_dim(decay_rate, co * 16 + zy * 2, 2, axis=1)
    weight = lax.dynamic_slice_in_dim(residue, co * 16 + zy * 2, 2, axis=1)
    gated = mixer(packed, taps, skip, decay, weight)
    gated = lax.all_to_all(
        gated.reshape(64, 32, 256), ("zl", "x", "zh", "y"), split_axis=0, concat_axis=0, tiled=True
    ).reshape(8, 256, 256)

    where = jnp.stack([x, y, zh * 2 + zl, co]).astype(jnp.int32)
    own, other = project(where, bucket_of_slot, gated, here, pieces)
    other = flip(other, "co", 1, 2)
    return (own + other.astype(F32)).astype(BF16)[None]


def solution(mesh):
    mesh = Mesh(mesh.devices.reshape(2, 4, 2, 2, 4), ("zh", "y", "co", "zl", "x"))
    in_specs = (
        P(DP, CTX),
        P(),
        P(DP, None, None),
        P(),
        P(DP, None, None, CTX),
        P(None, None, CTX),
        P(None, CTX),
        P(None, CTX),
        P(CTX),
        P(DP, None, CTX),
    )
    out_specs = P(DP, CTX, None)
    return jax.shard_map(body, mesh=mesh, in_specs=in_specs, out_specs=out_specs, check_vma=False)
```

```python
import jax
import jax.numpy as jnp
from jax import lax
from jax.experimental import pallas as pl
from jax.experimental.pallas import tpu as pltpu
from jax.sharding import Mesh
from jax.sharding import PartitionSpec as P

F32 = jnp.float32
BF16 = jnp.bfloat16
D = 4096
SEQ = 1024
EPS = 1e-06
DP = ("zh", "y", "co")
CTX = ("zl", "x")


def shift(value, axis, step):
    return lax.ppermute(value, axis, [(i, (i + step) % 4) for i in range(4)])


def flip(value, axes, bits, size):
    return lax.ppermute(value, axes, [(i, i ^ bits) for i in range(size)])


def mixer_kernel(recv, taps, skip, decay, residue, out, toep, prod, query):
    table = recv[0, 0:96, :].astype(F32)
    extra = recv[0, 96:112, :].astype(F32)
    square = extra[8:9] + extra[9:10]
    for i in range(1, 8):
        table = table + recv[i, 0:96, :].astype(F32)
        extra = recv[i, 96:112, :].astype(F32)
        square = square + extra[8:9] + extra[9:10]
    table = (table * lax.rsqrt(square / D + EPS)).astype(BF16)

    for g in range(2):
        time = lax.broadcasted_iota(jnp.int32, (16, SEQ), 1).astype(F32)
        terms = jnp.exp(-decay[:, g : g + 1] * time) * residue[:, g : g + 1]
        filt = jnp.sum(terms, axis=0, keepdims=True).astype(BF16).astype(F32)
        filt = jnp.concatenate([filt, jnp.zeros((1, 128), F32)], axis=1)
        lagged = pltpu.roll(
            jnp.broadcast_to(filt, (128, SEQ + 128)), 0, 1, stride=1, stride_axis=0
        ).astype(BF16)
        for k in range(4):
            toep[g, k, 0:128, :] = lagged[:, 256 * k : 256 * k + 256]
            if k == 0:
                toep[g, k, 128:256, 0:128] = jnp.zeros((128, 128), BF16)
                toep[g, k, 128:256, 128:256] = lagged[:, 0:128]
            else:
                toep[g, k, 128:256, :] = lagged[:, 256 * k - 128 : 256 * k + 128]

    vocab = lax.broadcasted_iota(jnp.int32, (512, 512), 0).astype(F32)
    lane = lax.broadcasted_iota(jnp.int32, (96, SEQ), 1)

    def one_pair(i, carry):
        extra = recv[i, 96:112, :].astype(F32)
        for j in range(2):
            parts = []
            for a in range(2):
                r = 2 * j + a
                ids = extra[r : r + 1] * 256.0 + extra[4 + r : 5 + r]
                hot = jnp.where(vocab == ids, 1.0, 0.0).astype(BF16)
                parts.append(jnp.dot(table, hot, preferred_element_type=F32))
            z0 = jnp.concatenate(parts, axis=1)
            z1 = jnp.where(lane >= 1, pltpu.roll(z0, 1, 1), 0.0)
            z2 = jnp.where(lane >= 2, pltpu.roll(z0, 2, 1), 0.0)
            f = taps[0] * z0 + taps[1] * z1 + taps[2] * z2
            u = (f[32:64] * f[64:96]).astype(BF16)
            rows = pl.ds(pl.multiple_of((2 * i + j) * 16, 16), 16)
            for g in range(2):
                for b in range(4):
                    cols = slice(256 * b, 256 * b + 256)
                    prod[g, b, rows, :] = u[16 * g : 16 * g + 16, cols]
                    query[g, b, rows, :] = f[16 * g : 16 * g + 16, cols]
        return carry

    lax.fori_loop(0, 8, one_pair, 0)

    for g in range(2):
        for b in range(4):
            mixed = skip[g] * prod[g, b].astype(F32)
            for a in range(b + 1):
                mixed = mixed + jnp.dot(prod[g, a], toep[g, b - a], preferred_element_type=F32)
            gated = (query[g, b] * mixed).astype(BF16)
            for n in range(16):
                for h in range(2):
                    out[
                        2 * b + h,
                        n // 2,
                        16 * g : 16 * g + 16,
                        128 * (n % 2) : 128 * (n % 2) + 128,
                    ] = gated[16 * n : 16 * n + 16, 128 * h : 128 * h + 128]


def mixer(recv, taps, skip, decay, residue):
    vmem = pl.BlockSpec(memory_space=pltpu.VMEM)
    return pl.pallas_call(
        mixer_kernel,
        out_shape=jax.ShapeDtypeStruct((8, 8, 32, 256), BF16),
        in_specs=[vmem] * 5,
        out_specs=vmem,
        scratch_shapes=[
            pltpu.VMEM((2, 4, 256, 256), BF16),
            pltpu.VMEM((2, 4, 256, 256), BF16),
            pltpu.VMEM((2, 4, 256, 256), F32),
        ],
        compiler_params=pltpu.CompilerParams(vmem_limit_bytes=32 << 20),
        cost_estimate=pl.CostEstimate(
            flops=2 * 16 * 96 * 512 * 1024, bytes_accessed=4 << 20, transcendentals=0
        ),
        name="mixer",
    )(recv, taps, skip, decay, residue)


def project_kernel(core, bucket, gated, ids, tiles, own, other):
    owner = pl.program_id(0)
    co = core[0]
    left = jnp.concatenate(
        [tiles[0, k // 4, 0, k % 4, :, 0:128].reshape(512, 256) for k in range(8)], axis=1
    )
    total = jnp.dot(left, gated[...], preferred_element_type=F32)
    lane = lax.broadcasted_iota(jnp.int32, (256, 256), 1)
    vocab = lane + (lane // 32) * 32 + co * 32
    hot = jnp.where(ids[...] == vocab, 1.0, 0.0).astype(BF16)
    for s in range(4):
        words = jnp.concatenate(
            [
                tiles[0, k // 4, 0, k % 4, s, 128:144, 128 * h : 128 * h + 128]
                for k in range(8)
                for h in range(2)
            ],
            axis=0,
        )
        looked = jnp.dot(hot, words, preferred_element_type=F32)
        both = total[128 * s : 128 * s + 128].T + looked
        slot = 4 * owner + 2 * (co if s < 2 else 1 - co) + s % 2
        cols = pl.ds(pl.multiple_of(bucket[slot] * 128, 128), 128)
        own[:, cols] = jnp.where(co == 0, both[0:128], both[128:256])
        other[:, cols] = jnp.where(co == 0, both[128:256], both[0:128]).astype(BF16)


def project(core, bucket, gated, ids, tiles):
    smem = pl.BlockSpec(memory_space=pltpu.SMEM)

    def whole(shape):
        return pl.BlockSpec(shape, lambda i: (0,) * len(shape))

    return pl.pallas_call(
        project_kernel,
        grid=(8,),
        out_shape=(
            jax.ShapeDtypeStruct((128, D), F32),
            jax.ShapeDtypeStruct((128, D), BF16),
        ),
        in_specs=[
            smem,
            smem,
            whole((2048, 256)),
            whole((256, 1)),
            pl.BlockSpec((1, 2, 1, 4, 4, 144, 256), lambda i: (i // 4, 0, i % 4, 0, 0, 0, 0)),
        ],
        out_specs=(whole((128, D)), whole((128, D))),
        compiler_params=pltpu.CompilerParams(vmem_limit_bytes=32 << 20),
        cost_estimate=pl.CostEstimate(
            flops=2 * 256 * 4096 * 2048, bytes_accessed=24 << 20, transcendentals=0
        ),
        name="project",
    )(core, bucket, gated, ids, tiles)


def body(
    token_ids,
    bucket_of_slot,
    embed_tiles,
    norm_gain,
    in_tiles,
    short_taps,
    decay_rate,
    residue,
    skip_gain,
    out_tiles,
):
    zh, y, co, zl, x = (lax.axis_index(a) for a in ("zh", "y", "co", "zl", "x"))
    zy = zh * 4 + y
    c = zl * 4 + x
    d = zy * 2 + co

    def tile_for(core):
        rows = lax.dynamic_slice_in_dim(out_tiles, core * 256, 256, axis=2)
        words = lax.dynamic_slice_in_dim(embed_tiles, (c * 2 + core) * 32, 32, axis=1)
        words = words.reshape(2, 2, 16, 128).transpose(0, 2, 1, 3).reshape(2, 16, 256)
        return jnp.concatenate([rows, words], axis=1)

    tiles = jnp.concatenate([tile_for(co), flip(tile_for(1 - co), "co", 1, 2)])
    tiles = lax.all_gather(tiles, ("zh", "zl", "y", "x"), axis=0, tiled=True)
    tiles = tiles.reshape(2, 2, 4, 4, 4, 144, 256)

    core_index = lax.broadcasted_iota(jnp.int32, (2, 8, 128), 0)
    ctx_index = lax.broadcasted_iota(jnp.int32, (2, 8, 128), 1)
    ids = jnp.where((core_index == co) & (ctx_index == c), token_ids[None], 0)
    ids = ids + shift(ids, "x", 1) + shift(ids, "x", -1) + shift(ids, "x", 2)
    ids = ids + sum(flip(ids, ("co", "zl"), b, 4) for b in (1, 2, 3))
    here = lax.dynamic_index_in_dim(ids, c, 1, keepdims=False).reshape(256, 1)
    ids = ids.reshape(4, 512)
    ids_rows = jnp.concatenate([ids // 256, ids % 256]).astype(BF16)

    buckets = lax.dynamic_slice_in_dim(bucket_of_slot, 2 * d, 2)
    gain = jnp.take(norm_gain.reshape(32, 128), buckets, axis=0)
    embed_f32 = embed_tiles.astype(F32)
    scaled = (embed_f32 * gain[:, None, :]).astype(BF16)
    square = jnp.sum(embed_f32 * embed_f32, axis=(0, 2))
    high = lax.reduce_precision(square, 8, 7)
    square_rows = jnp.stack([high, square - high]).astype(BF16)

    def partial_for(core):
        weights = lax.dynamic_slice_in_dim(in_tiles, core * 256, 256, axis=3)
        weights = weights.reshape(2, 128, 3, 8, 32).transpose(0, 1, 3, 2, 4).reshape(2, 128, 768)
        return lax.dot_general(
            weights, scaled, (((0, 1), (0, 2)), ((), ())), preferred_element_type=F32
        )

    given = jnp.concatenate(
        [partial_for(1 - co).astype(BF16), square_rows, jnp.zeros((14, 512), BF16)]
    )
    taken = flip(given, "co", 1, 2).astype(F32)
    table = (partial_for(co) + taken[:768]).astype(BF16).reshape(8, 96, 512)
    square = square + taken[768] + taken[769]
    high = lax.reduce_precision(square, 8, 7)
    square_rows = jnp.stack([high, square - high]).astype(BF16)
    extra = jnp.concatenate([ids_rows, square_rows, jnp.zeros((6, 512), BF16)])
    packed = jnp.concatenate([table, jnp.broadcast_to(extra[None], (8, 16, 512))], axis=1)
    packed = lax.all_to_all(packed, ("zh", "y"), split_axis=0, concat_axis=0, tiled=True)

    first = co * 256 + zy * 32
    taps = lax.dynamic_slice_in_dim(short_taps, first, 32, axis=2).reshape(3, 96, 1)
    skip = lax.dynamic_slice_in_dim(skip_gain, first, 32).reshape(2, 1, 16)
    skip = jnp.broadcast_to(skip, (2, 16, 16)).reshape(2, 256, 1)
    decay = lax.dynamic_slice_in_dim(decay_rate, co * 16 + zy * 2, 2, axis=1)
    weight = lax.dynamic_slice_in_dim(residue, co * 16 + zy * 2, 2, axis=1)
    gated = mixer(packed, taps, skip, decay, weight)
    gated = lax.all_to_all(
        gated.reshape(64, 32, 256), ("zl", "x", "zh", "y"), split_axis=0, concat_axis=0, tiled=True
    ).reshape(2048, 256)

    core = jnp.reshape(co, (1,)).astype(jnp.int32)
    own, other = project(core, bucket_of_slot, gated, here, tiles)
    other = flip(other, "co", 1, 2)
    return (own + other.astype(F32)).astype(BF16)[None]


def solution(mesh):
    mesh = Mesh(mesh.devices.reshape(2, 4, 2, 2, 4), ("zh", "y", "co", "zl", "x"))
    in_specs = (
        P(DP, CTX),
        P(),
        P(DP, None, None),
        P(),
        P(DP, None, None, CTX),
        P(None, None, CTX),
        P(None, CTX),
        P(None, CTX),
        P(CTX),
        P(DP, None, CTX),
    )
    out_specs = P(DP, CTX, None)
    return jax.shard_map(body, mesh=mesh, in_specs=in_specs, out_specs=out_specs, check_vma=False)
```

```python
import functools

import jax
import jax.numpy as jnp
from jax import lax
from jax.experimental import pallas as pl
from jax.experimental.pallas import tpu as pltpu
from jax.sharding import Mesh
from jax.sharding import PartitionSpec as P

F32 = jnp.float32
BF16 = jnp.bfloat16
D = 4096
SEQ = 1024
EPS = 1e-06
OFFSETS = (0, 3, 1, 2)
DP = ("zh", "y", "co")
CTX = ("zl", "x")


def shift(value, axis, step):
    return lax.ppermute(value, axis, [(i, (i + step) % 4) for i in range(4)])


def flip(value, axes, bits, size):
    return lax.ppermute(value, axes, [(i, i ^ bits) for i in range(size)])


def rings(values, axes, after=()):
    near = []
    for value, axis in zip(values, axes):
        near += [shift(value, axis, 1), shift(value, axis, -1)]
    near = lax.optimization_barrier((*near, *after))[:4]
    far = []
    for i, axis in enumerate(axes):
        half = values[i].shape[0] // 2
        far += [shift(near[2 * i][:half], axis, 1), shift(near[2 * i + 1][half:], axis, -1)]
    far = lax.optimization_barrier(tuple(far))
    return [(values[i], *near[2 * i : 2 * i + 2], *far[2 * i : 2 * i + 2]) for i in range(2)]


def filter_kernel(decay, residue, toep):
    for g in range(2):
        time = lax.broadcasted_iota(jnp.int32, (16, SEQ), 1).astype(F32)
        terms = jnp.exp(-decay[:, g : g + 1] * time) * residue[:, g : g + 1]
        filt = jnp.sum(terms, axis=0, keepdims=True).astype(BF16).astype(F32)
        filt = jnp.concatenate([filt, jnp.zeros((1, 128), F32)], axis=1)
        lagged = pltpu.roll(
            jnp.broadcast_to(filt, (128, SEQ + 128)), 0, 1, stride=1, stride_axis=0
        ).astype(BF16)
        for k in range(4):
            toep[g, k, 0:128, :] = lagged[:, 256 * k : 256 * k + 256]
            if k == 0:
                toep[g, k, 128:256, 0:128] = jnp.zeros((128, 128), BF16)
                toep[g, k, 128:256, 128:256] = lagged[:, 0:128]
            else:
                toep[g, k, 128:256, :] = lagged[:, 256 * k - 128 : 256 * k + 128]


def filters(decay, residue):
    vmem = pl.BlockSpec(memory_space=pltpu.VMEM)
    return pl.pallas_call(
        filter_kernel,
        out_shape=jax.ShapeDtypeStruct((2, 4, 256, 256), BF16),
        in_specs=[vmem] * 2,
        out_specs=vmem,
        name="filters",
    )(decay, residue)


def mixer_kernel(recv, taps, skip, toep, out, prod, query):
    table = recv[0, 0:96, :].astype(F32)
    extra = recv[0, 96:112, :].astype(F32)
    square = extra[8:9] + extra[9:10]
    for i in range(1, 8):
        table = table + recv[i, 0:96, :].astype(F32)
        extra = recv[i, 96:112, :].astype(F32)
        square = square + extra[8:9] + extra[9:10]
    table = (table * lax.rsqrt(square / D + EPS)).astype(BF16)

    vocab = lax.broadcasted_iota(jnp.int32, (512, 512), 0).astype(F32)
    lane = lax.broadcasted_iota(jnp.int32, (96, SEQ), 1)

    def one_pair(i, carry):
        extra = recv[i, 96:112, :].astype(F32)
        for j in range(2):
            parts = []
            for a in range(2):
                r = 2 * j + a
                ids = extra[r : r + 1] * 256.0 + extra[4 + r : 5 + r]
                hot = jnp.where(vocab == ids, 1.0, 0.0).astype(BF16)
                parts.append(jnp.dot(table, hot, preferred_element_type=F32))
            z0 = jnp.concatenate(parts, axis=1)
            z1 = jnp.where(lane >= 1, pltpu.roll(z0, 1, 1), 0.0)
            z2 = jnp.where(lane >= 2, pltpu.roll(z0, 2, 1), 0.0)
            f = taps[0] * z0 + taps[1] * z1 + taps[2] * z2
            u = (f[32:64] * f[64:96]).astype(BF16)
            rows = pl.ds(pl.multiple_of((2 * i + j) * 16, 16), 16)
            for g in range(2):
                for b in range(4):
                    cols = slice(256 * b, 256 * b + 256)
                    prod[g, b, rows, :] = u[16 * g : 16 * g + 16, cols]
                    query[g, b, rows, :] = f[16 * g : 16 * g + 16, cols]
        return carry

    lax.fori_loop(0, 8, one_pair, 0)

    for g in range(2):
        for b in range(4):
            mixed = skip[g] * prod[g, b].astype(F32)
            for a in range(b + 1):
                mixed = mixed + jnp.dot(prod[g, a], toep[g, b - a], preferred_element_type=F32)
            gated = (query[g, b] * mixed).astype(BF16)
            for n in range(16):
                for h in range(2):
                    c = 2 * b + h
                    lanes = 256 * (n % 2) + 128 * (c // 4)
                    out[c % 4, n // 2, 16 * g : 16 * g + 16, lanes : lanes + 128] = gated[
                        16 * n : 16 * n + 16, 128 * h : 128 * h + 128
                    ]


def mixer(recv, taps, skip, toep):
    vmem = pl.BlockSpec(memory_space=pltpu.VMEM)
    return pl.pallas_call(
        mixer_kernel,
        out_shape=jax.ShapeDtypeStruct((4, 8, 32, 512), BF16),
        in_specs=[vmem] * 4,
        out_specs=vmem,
        scratch_shapes=[
            pltpu.VMEM((2, 4, 256, 256), BF16),
            pltpu.VMEM((2, 4, 256, 256), F32),
        ],
        compiler_params=pltpu.CompilerParams(vmem_limit_bytes=32 << 20),
        cost_estimate=pl.CostEstimate(
            flops=2 * 16 * 96 * 512 * 1024, bytes_accessed=4 << 20, transcendentals=0
        ),
        name="mixer",
    )(recv, taps, skip, toep)


def project_kernel(far_axis, where, gated, ids, *refs):
    pieces = refs[:5]
    mine, theirs, right, hot = refs[5:]
    x, y, zl, co = where[0], where[1], where[3], where[4]

    for r in range(4):
        x_of = lax.rem(x + OFFSETS[r], 4)
        right[256 * r : 256 * r + 256, :] = gated[x_of]
        word = lax.broadcasted_iota(jnp.int32, (32, 512), 0) + ((zl * 4 + x_of) * 2 + co) * 32
        hot[32 * r : 32 * r + 32, :] = jnp.where(word == ids[...], 1.0, 0.0).astype(BF16)

    def block(xr, yr, s):
        near, far = (xr, yr) if far_axis == "y" else (yr, xr)
        at = 4 * near + s
        if far < 3:
            return pieces[far].at[at]
        return pieces[3].at[at] if at < 8 else pieces[4].at[at - 8]

    for yr in range(4):
        y_of = lax.rem(y + OFFSETS[yr], 4)
        for s in range(4):
            tiles = [block(xr, yr, s) for xr in range(4)]
            rows = jnp.concatenate([t[0:128, :] for t in tiles], axis=1)
            words = jnp.concatenate(
                [t[128:144, 128 * h : 128 * h + 128] for t in tiles for h in range(2)], axis=0
            )
            total = jnp.dot(rows, right[...], preferred_element_type=F32)
            total = total + lax.dot_general(
                words, hot[...], (((0,), (0,)), ((), ())), preferred_element_type=F32
            )
            cols = slice(128 * s, 128 * s + 128)
            mine[y_of, cols, :] = jnp.where(co == 0, total[:, 0:256], total[:, 256:512])
            theirs[y_of, cols, :] = jnp.where(
                co == 0, total[:, 256:512], total[:, 0:256]
            ).astype(BF16)


def project(far_axis, where, gated, ids, pieces):
    vmem = pl.BlockSpec(memory_space=pltpu.VMEM)
    smem = pl.BlockSpec(memory_space=pltpu.SMEM)
    return pl.pallas_call(
        functools.partial(project_kernel, far_axis),
        out_shape=(
            jax.ShapeDtypeStruct((4, 512, 256), F32),
            jax.ShapeDtypeStruct((4, 512, 256), BF16),
        ),
        in_specs=[smem] + [vmem] * 7,
        out_specs=(vmem, vmem),
        scratch_shapes=[pltpu.VMEM((1024, 512), BF16), pltpu.VMEM((128, 512), BF16)],
        compiler_params=pltpu.CompilerParams(vmem_limit_bytes=32 << 20),
        cost_estimate=pl.CostEstimate(
            flops=2 * 512 * 2048 * 1024, bytes_accessed=10 << 20, transcendentals=0
        ),
        name="project_" + far_axis,
    )(where, gated, ids, *pieces)


def merge_kernel(where, mine, theirs, keep, give):
    zl = where[3]
    for y in range(4):
        total = mine[y] + theirs[y].astype(F32)
        low, high = total[:, 0:128], total[:, 128:256]
        keep[y] = jnp.where(zl == 0, low, high)
        give[y] = jnp.where(zl == 0, high, low).astype(BF16)


def merge(where, mine, theirs):
    vmem = pl.BlockSpec(memory_space=pltpu.VMEM)
    smem = pl.BlockSpec(memory_space=pltpu.SMEM)
    return pl.pallas_call(
        merge_kernel,
        out_shape=(
            jax.ShapeDtypeStruct((4, 512, 128), F32),
            jax.ShapeDtypeStruct((4, 512, 128), BF16),
        ),
        in_specs=[smem, vmem, vmem],
        out_specs=(vmem, vmem),
        compiler_params=pltpu.CompilerParams(vmem_limit_bytes=16 << 20),
        name="merge",
    )(where, mine, theirs)


def finish_kernel(where, bucket, keep0, keep1, got0, got1, out):
    zh = where[2]
    for p, (keep, got) in enumerate(((keep0, got0), (keep1, got1))):
        for y in range(4):
            for s in range(4):
                rows = slice(128 * s, 128 * s + 128)
                total = keep[y, rows, :] + got[y, rows, :].astype(F32)
                slot = 16 * lax.rem(zh + p, 2) + 4 * y + s
                cols = pl.ds(pl.multiple_of(bucket[slot] * 128, 128), 128)
                out[:, cols] = total.T.astype(BF16)


def finish(where, bucket, keep, got):
    vmem = pl.BlockSpec(memory_space=pltpu.VMEM)
    smem = pl.BlockSpec(memory_space=pltpu.SMEM)
    return pl.pallas_call(
        finish_kernel,
        out_shape=jax.ShapeDtypeStruct((128, D), BF16),
        in_specs=[smem, smem] + [vmem] * 4,
        out_specs=vmem,
        compiler_params=pltpu.CompilerParams(vmem_limit_bytes=24 << 20),
        name="finish",
    )(where, bucket, *keep, *got)


def body(
    token_ids,
    bucket_of_slot,
    embed_tiles,
    norm_gain,
    in_tiles,
    short_taps,
    decay_rate,
    residue,
    skip_gain,
    out_tiles,
):
    zh, y, co, zl, x = (lax.axis_index(a) for a in ("zh", "y", "co", "zl", "x"))
    zy = zh * 4 + y
    c = zl * 4 + x
    d = zy * 2 + co

    core_index = lax.broadcasted_iota(jnp.int32, (2, 8, 128), 0)
    ctx_index = lax.broadcasted_iota(jnp.int32, (2, 8, 128), 1)
    ids = jnp.where((core_index == co) & (ctx_index == c), token_ids[None], 0)
    ids = ids + shift(ids, "x", 1) + shift(ids, "x", -1) + shift(ids, "x", 2)
    ids, in_tiles = lax.optimization_barrier((ids, in_tiles))
    ids = ids + sum(flip(ids, ("co", "zl"), b, 4) for b in (1, 2, 3))
    here = lax.dynamic_index_in_dim(ids.reshape(2, 2, 4, 128), x, 2, keepdims=False)
    here = here.reshape(1, 512)
    ids = ids.reshape(4, 512)
    ids_rows = jnp.concatenate([ids // 256, ids % 256]).astype(BF16)

    def tile_for(core):
        rows = lax.dynamic_slice_in_dim(out_tiles, core * 256, 256, axis=2)
        words = lax.dynamic_slice_in_dim(embed_tiles, (c * 2 + core) * 32, 32, axis=1)
        words = words.reshape(2, 2, 16, 128).transpose(0, 2, 1, 3).reshape(2, 16, 256)
        return jnp.concatenate([rows, words], axis=1)

    ours, sent = tile_for(co), flip(tile_for(1 - co), "co", 1, 2)
    tiles = jnp.concatenate([jnp.where(co == 0, ours, sent), jnp.where(co == 0, sent, ours)])
    across = flip(tiles, "zh", 1, 2)

    buckets = lax.dynamic_slice_in_dim(bucket_of_slot, 2 * d, 2)
    gain = jnp.take(norm_gain.reshape(32, 128), buckets, axis=0)
    embed_f32 = embed_tiles.astype(F32)
    scaled = (embed_f32 * gain[:, None, :]).astype(BF16)
    square = jnp.sum(embed_f32 * embed_f32, axis=(0, 2))
    high = lax.reduce_precision(square, 8, 7)
    square_rows = jnp.stack([high, square - high]).astype(BF16)

    def partial_for(core):
        weights = lax.dynamic_slice_in_dim(in_tiles, core * 256, 256, axis=3).reshape(2, 128, 768)
        return lax.dot_general(
            weights, scaled, (((0, 1), (0, 2)), ((), ())), preferred_element_type=F32
        )

    given = jnp.concatenate(
        [partial_for(1 - co).astype(BF16), square_rows, jnp.zeros((14, 512), BF16)]
    )
    taken = flip(given, "co", 1, 2).astype(F32)
    table = (partial_for(co) + taken[:768]).astype(BF16).reshape(3, 8, 32, 512)
    square = square + taken[768] + taken[769]
    high = lax.reduce_precision(square, 8, 7)
    square_rows = jnp.stack([high, square - high]).astype(BF16)
    extra = jnp.concatenate([ids_rows, square_rows, jnp.zeros((6, 512), BF16)])
    packed = jnp.concatenate(
        [table[0], table[1], table[2], jnp.broadcast_to(extra[None], (8, 16, 512))], axis=1
    )
    parts = rings((tiles, across), ("x", "y"), (packed,))
    parts = [jnp.concatenate(blocks) for blocks in parts]
    pieces = rings(parts, ("y", "x"))

    packed = lax.all_to_all(packed, ("zh", "y"), split_axis=0, concat_axis=0, tiled=True)

    first = co * 256 + zy * 32
    taps = lax.dynamic_slice_in_dim(short_taps, first, 32, axis=2).reshape(3, 96, 1)
    skip = lax.dynamic_slice_in_dim(skip_gain, first, 32).reshape(2, 1, 16)
    skip = jnp.broadcast_to(skip, (2, 16, 16)).reshape(2, 256, 1)
    decay = lax.dynamic_slice_in_dim(decay_rate, co * 16 + zy * 2, 2, axis=1)
    weight = lax.dynamic_slice_in_dim(residue, co * 16 + zy * 2, 2, axis=1)
    gated = mixer(packed, taps, skip, filters(decay, weight))
    gated = lax.all_to_all(
        gated.reshape(32, 32, 512), ("x", "zh", "y"), split_axis=0, concat_axis=0, tiled=True
    ).reshape(4, 256, 512)

    where = jnp.stack([x, y, zh, zl, co]).astype(jnp.int32)
    keep, got = [], []
    for p, far in enumerate(("y", "x")):
        mine, theirs = project(far, where, gated, here, pieces[p])
        kept, given = merge(where, mine, flip(theirs, "co", 1, 2))
        keep.append(kept)
        got.append(flip(given, "zl", 1, 2))
    return finish(where, bucket_of_slot, keep, got)[None]


def solution(mesh):
    mesh = Mesh(mesh.devices.reshape(2, 4, 2, 2, 4), ("zh", "y", "co", "zl", "x"))
    in_specs = (
        P(DP, CTX),
        P(),
        P(DP, None, None),
        P(),
        P(DP, None, None, CTX),
        P(None, None, CTX),
        P(None, CTX),
        P(None, CTX),
        P(CTX),
        P(DP, None, CTX),
    )
    out_specs = P(DP, CTX, None)
    return jax.shard_map(body, mesh=mesh, in_specs=in_specs, out_specs=out_specs, check_vma=False)
```

```python
import functools

import jax
import jax.numpy as jnp
from jax import lax
from jax.experimental import pallas as pl
from jax.experimental.pallas import tpu as pltpu
from jax.sharding import Mesh
from jax.sharding import PartitionSpec as P

F32 = jnp.float32
BF16 = jnp.bfloat16
D = 4096
SEQ = 1024
EPS = 1e-06
OFFSETS = (0, 3, 1, 2)
DP = ("zh", "y", "co")
CTX = ("zl", "x")


def shift(value, axis, step):
    return lax.ppermute(value, axis, [(i, (i + step) % 4) for i in range(4)])


def flip(value, axes, bits, size):
    return lax.ppermute(value, axes, [(i, i ^ bits) for i in range(size)])


def rings(values, axes, after=()):
    near = []
    for value, axis in zip(values, axes):
        near += [shift(value, axis, 1), shift(value, axis, -1)]
    near = lax.optimization_barrier((*near, *after))[:4]
    far = []
    for i, axis in enumerate(axes):
        half = values[i].shape[0] // 2
        far += [shift(near[2 * i][:half], axis, 1), shift(near[2 * i + 1][half:], axis, -1)]
    far = lax.optimization_barrier(tuple(far))
    return [(values[i], *near[2 * i : 2 * i + 2], *far[2 * i : 2 * i + 2]) for i in range(2)]


def filter_kernel(decay, residue, toep):
    for g in range(2):
        time = lax.broadcasted_iota(jnp.int32, (16, SEQ), 1).astype(F32)
        terms = jnp.exp(-decay[:, g : g + 1] * time) * residue[:, g : g + 1]
        filt = jnp.sum(terms, axis=0, keepdims=True).astype(BF16).astype(F32)
        filt = jnp.concatenate([filt, jnp.zeros((1, 128), F32)], axis=1)
        lagged = pltpu.roll(
            jnp.broadcast_to(filt, (128, SEQ + 128)), 0, 1, stride=1, stride_axis=0
        ).astype(BF16)
        for k in range(4):
            toep[g, k, 0:128, :] = lagged[:, 256 * k : 256 * k + 256]
            if k == 0:
                toep[g, k, 128:256, 0:128] = jnp.zeros((128, 128), BF16)
                toep[g, k, 128:256, 128:256] = lagged[:, 0:128]
            else:
                toep[g, k, 128:256, :] = lagged[:, 256 * k - 128 : 256 * k + 128]


def filters(decay, residue):
    vmem = pl.BlockSpec(memory_space=pltpu.VMEM)
    return pl.pallas_call(
        filter_kernel,
        out_shape=jax.ShapeDtypeStruct((2, 4, 256, 256), BF16),
        in_specs=[vmem] * 2,
        out_specs=vmem,
        name="filters",
    )(decay, residue)


def mixer_kernel(recv, taps, skip, toep, out, prod, query):
    table = recv[0, 0:96, :].astype(F32)
    extra = recv[0, 96:112, :].astype(F32)
    square = extra[8:9] + extra[9:10]
    for i in range(1, 8):
        table = table + recv[i, 0:96, :].astype(F32)
        extra = recv[i, 96:112, :].astype(F32)
        square = square + extra[8:9] + extra[9:10]
    table = (table * lax.rsqrt(square / D + EPS)).astype(BF16)

    vocab = lax.broadcasted_iota(jnp.int32, (512, 512), 0).astype(F32)
    lane = lax.broadcasted_iota(jnp.int32, (96, SEQ), 1)

    def one_pair(i, carry):
        extra = recv[i, 96:112, :].astype(F32)
        for j in range(2):
            parts = []
            for a in range(2):
                r = 2 * j + a
                ids = extra[r : r + 1] * 256.0 + extra[4 + r : 5 + r]
                hot = jnp.where(vocab == ids, 1.0, 0.0).astype(BF16)
                parts.append(jnp.dot(table, hot, preferred_element_type=F32))
            z0 = jnp.concatenate(parts, axis=1)
            z1 = jnp.where(lane >= 1, pltpu.roll(z0, 1, 1), 0.0)
            z2 = jnp.where(lane >= 2, pltpu.roll(z0, 2, 1), 0.0)
            f = taps[0] * z0 + taps[1] * z1 + taps[2] * z2
            u = (f[32:64] * f[64:96]).astype(BF16)
            rows = pl.ds(pl.multiple_of((2 * i + j) * 16, 16), 16)
            for g in range(2):
                for b in range(4):
                    cols = slice(256 * b, 256 * b + 256)
                    prod[g, b, rows, :] = u[16 * g : 16 * g + 16, cols]
                    query[g, b, rows, :] = f[16 * g : 16 * g + 16, cols]
        return carry

    lax.fori_loop(0, 8, one_pair, 0)

    for g in range(2):
        for b in range(4):
            mixed = skip[g] * prod[g, b].astype(F32)
            for a in range(b + 1):
                mixed = mixed + jnp.dot(prod[g, a], toep[g, b - a], preferred_element_type=F32)
            gated = (query[g, b] * mixed).astype(BF16)
            for n in range(16):
                for h in range(2):
                    c = 2 * b + h
                    lanes = 256 * (n % 2) + 128 * (c // 4)
                    out[c % 4, n // 2, 16 * g : 16 * g + 16, lanes : lanes + 128] = gated[
                        16 * n : 16 * n + 16, 128 * h : 128 * h + 128
                    ]


def mixer(recv, taps, skip, toep):
    vmem = pl.BlockSpec(memory_space=pltpu.VMEM)
    return pl.pallas_call(
        mixer_kernel,
        out_shape=jax.ShapeDtypeStruct((4, 8, 32, 512), BF16),
        in_specs=[vmem] * 4,
        out_specs=vmem,
        scratch_shapes=[
            pltpu.VMEM((2, 4, 256, 256), BF16),
            pltpu.VMEM((2, 4, 256, 256), F32),
        ],
        compiler_params=pltpu.CompilerParams(vmem_limit_bytes=32 << 20),
        cost_estimate=pl.CostEstimate(
            flops=2 * 16 * 96 * 512 * 1024, bytes_accessed=4 << 20, transcendentals=0
        ),
        name="mixer",
    )(recv, taps, skip, toep)


def front_block(refs, i, xr, s):
    return refs[i].at[4 * xr + s]


def back_block(refs, i, xr, s):
    if i == 0:
        return refs[xr // 2].at[4 * (xr % 2) + s]
    at = 4 * (i - 1) + s
    return refs[2 + xr].at[at] if xr < 3 else refs[5 + at // 8].at[at % 8]


def project_kernel(count, block, where, gated, ids, *refs):
    mine, theirs, right, hot = refs[-4:]
    x, zl, co = where[0], where[3], where[4]

    for r in range(4):
        x_of = lax.rem(x + OFFSETS[r], 4)
        right[256 * r : 256 * r + 256, :] = gated[x_of]
        word = lax.broadcasted_iota(jnp.int32, (32, 512), 0) + ((zl * 4 + x_of) * 2 + co) * 32
        hot[32 * r : 32 * r + 32, :] = jnp.where(word == ids[...], 1.0, 0.0).astype(BF16)

    for i in range(count):
        for s in range(4):
            tiles = [block(refs, i, xr, s) for xr in range(4)]
            rows = jnp.concatenate([t[0:128, :] for t in tiles], axis=1)
            words = jnp.concatenate(
                [t[128:144, 128 * h : 128 * h + 128] for t in tiles for h in range(2)], axis=0
            )
            total = jnp.dot(rows, right[...], preferred_element_type=F32)
            total = total + lax.dot_general(
                words, hot[...], (((0,), (0,)), ((), ())), preferred_element_type=F32
            )
            cols = slice(128 * s, 128 * s + 128)
            mine[i, cols, :] = jnp.where(co == 0, total[:, 0:256], total[:, 256:512])
            theirs[i, cols, :] = jnp.where(co == 0, total[:, 256:512], total[:, 0:256]).astype(
                BF16
            )


def project(name, count, block, where, gated, ids, pieces):
    vmem = pl.BlockSpec(memory_space=pltpu.VMEM)
    smem = pl.BlockSpec(memory_space=pltpu.SMEM)
    return pl.pallas_call(
        functools.partial(project_kernel, count, block),
        out_shape=(
            jax.ShapeDtypeStruct((count, 512, 256), F32),
            jax.ShapeDtypeStruct((count, 512, 256), BF16),
        ),
        in_specs=[smem] + [vmem] * (2 + len(pieces)),
        out_specs=(vmem, vmem),
        scratch_shapes=[pltpu.VMEM((1024, 512), BF16), pltpu.VMEM((128, 512), BF16)],
        compiler_params=pltpu.CompilerParams(vmem_limit_bytes=32 << 20),
        cost_estimate=pl.CostEstimate(
            flops=2 * 512 * 512 * count * 1024, bytes_accessed=3 * count << 20, transcendentals=0
        ),
        name=name,
    )(where, gated, ids, *pieces)


def merge_kernel(where, mine, theirs, keep, give):
    zl = where[3]
    for i in range(mine.shape[0]):
        total = mine[i] + theirs[i].astype(F32)
        low, high = total[:, 0:128], total[:, 128:256]
        keep[i] = jnp.where(zl == 0, low, high)
        give[i] = jnp.where(zl == 0, high, low).astype(BF16)


def merge(where, mine, theirs):
    vmem = pl.BlockSpec(memory_space=pltpu.VMEM)
    smem = pl.BlockSpec(memory_space=pltpu.SMEM)
    return pl.pallas_call(
        merge_kernel,
        out_shape=(
            jax.ShapeDtypeStruct((mine.shape[0], 512, 128), F32),
            jax.ShapeDtypeStruct((mine.shape[0], 512, 128), BF16),
        ),
        in_specs=[smem, vmem, vmem],
        out_specs=(vmem, vmem),
        compiler_params=pltpu.CompilerParams(vmem_limit_bytes=16 << 20),
        name="merge",
    )(where, mine, theirs)


def finish_kernel(where, bucket, keep0, keep1, got0, got1, out):
    y, zh = where[1], where[2]
    for p in range(2):
        for r in range(4):
            keep, got, i = (keep0, got0, r) if p == 0 and r < 3 else (keep1, got1, p * (r + 1))
            for s in range(4):
                rows = slice(128 * s, 128 * s + 128)
                total = keep[i, rows, :] + got[i, rows, :].astype(F32)
                slot = 16 * lax.rem(zh + p, 2) + 4 * lax.rem(y + OFFSETS[r], 4) + s
                cols = pl.ds(pl.multiple_of(bucket[slot] * 128, 128), 128)
                out[:, cols] = total.T.astype(BF16)


def finish(where, bucket, keep, got):
    vmem = pl.BlockSpec(memory_space=pltpu.VMEM)
    smem = pl.BlockSpec(memory_space=pltpu.SMEM)
    return pl.pallas_call(
        finish_kernel,
        out_shape=jax.ShapeDtypeStruct((128, D), BF16),
        in_specs=[smem, smem] + [vmem] * 4,
        out_specs=vmem,
        compiler_params=pltpu.CompilerParams(vmem_limit_bytes=24 << 20),
        name="finish",
    )(where, bucket, *keep, *got)


def body(
    token_ids,
    bucket_of_slot,
    embed_tiles,
    norm_gain,
    in_tiles,
    short_taps,
    decay_rate,
    residue,
    skip_gain,
    out_tiles,
):
    zh, y, co, zl, x = (lax.axis_index(a) for a in ("zh", "y", "co", "zl", "x"))
    zy = zh * 4 + y
    c = zl * 4 + x
    d = zy * 2 + co

    core_index = lax.broadcasted_iota(jnp.int32, (2, 8, 128), 0)
    ctx_index = lax.broadcasted_iota(jnp.int32, (2, 8, 128), 1)
    ids = jnp.where((core_index == co) & (ctx_index == c), token_ids[None], 0)
    ids = ids + shift(ids, "x", 1) + shift(ids, "x", -1) + shift(ids, "x", 2)
    ids, in_tiles = lax.optimization_barrier((ids, in_tiles))
    ids = ids + sum(flip(ids, ("co", "zl"), b, 4) for b in (1, 2, 3))
    here = lax.dynamic_index_in_dim(ids.reshape(2, 2, 4, 128), x, 2, keepdims=False)
    here = here.reshape(1, 512)
    ids = ids.reshape(4, 512)
    ids_rows = jnp.concatenate([ids // 256, ids % 256]).astype(BF16)

    def tile_for(core):
        rows = lax.dynamic_slice_in_dim(out_tiles, core * 256, 256, axis=2)
        words = lax.dynamic_slice_in_dim(embed_tiles, (c * 2 + core) * 32, 32, axis=1)
        words = words.reshape(2, 2, 16, 128).transpose(0, 2, 1, 3).reshape(2, 16, 256)
        return jnp.concatenate([rows, words], axis=1)

    ours, lent = tile_for(co), tile_for(1 - co)

    def by_core(own, sibling):
        return jnp.concatenate([jnp.where(co == 0, own, sibling), jnp.where(co == 0, sibling, own)])

    tiles = by_core(ours, flip(lent, "co", 1, 2))
    across = by_core(flip(ours, "zh", 1, 2), flip(lent, ("zh", "co"), 3, 4))

    buckets = lax.dynamic_slice_in_dim(bucket_of_slot, 2 * d, 2)
    gain = jnp.take(norm_gain.reshape(32, 128), buckets, axis=0)
    embed_f32 = embed_tiles.astype(F32)
    scaled = (embed_f32 * gain[:, None, :]).astype(BF16)
    square = jnp.sum(embed_f32 * embed_f32, axis=(0, 2))
    high = lax.reduce_precision(square, 8, 7)
    square_rows = jnp.stack([high, square - high]).astype(BF16)

    def partial_for(core):
        weights = lax.dynamic_slice_in_dim(in_tiles, core * 256, 256, axis=3).reshape(2, 128, 768)
        return lax.dot_general(
            weights, scaled, (((0, 1), (0, 2)), ((), ())), preferred_element_type=F32
        )

    given = jnp.concatenate(
        [partial_for(1 - co).astype(BF16), square_rows, jnp.zeros((14, 512), BF16)]
    )
    taken = flip(given, "co", 1, 2).astype(F32)
    table = (partial_for(co) + taken[:768]).astype(BF16).reshape(3, 8, 32, 512)
    square = square + taken[768] + taken[769]
    high = lax.reduce_precision(square, 8, 7)
    square_rows = jnp.stack([high, square - high]).astype(BF16)
    extra = jnp.concatenate([ids_rows, square_rows, jnp.zeros((6, 512), BF16)])
    packed = jnp.concatenate(
        [table[0], table[1], table[2], jnp.broadcast_to(extra[None], (8, 16, 512))], axis=1
    )
    parts = rings((tiles, across), ("x", "y"), (packed,))
    parts = [jnp.concatenate(blocks) for blocks in parts]
    pieces = rings(parts, ("y", "x"))

    packed = lax.all_to_all(packed, ("zh", "y"), split_axis=0, concat_axis=0, tiled=True)

    first = co * 256 + zy * 32
    taps = lax.dynamic_slice_in_dim(short_taps, first, 32, axis=2).reshape(3, 96, 1)
    skip = lax.dynamic_slice_in_dim(skip_gain, first, 32).reshape(2, 1, 16)
    skip = jnp.broadcast_to(skip, (2, 16, 16)).reshape(2, 256, 1)
    decay = lax.dynamic_slice_in_dim(decay_rate, co * 16 + zy * 2, 2, axis=1)
    weight = lax.dynamic_slice_in_dim(residue, co * 16 + zy * 2, 2, axis=1)
    gated = mixer(packed, taps, skip, filters(decay, weight))
    gated = lax.all_to_all(
        gated.reshape(32, 32, 512), ("x", "zh", "y"), split_axis=0, concat_axis=0, tiled=True
    ).reshape(4, 256, 512)

    where = jnp.stack([x, y, zh, zl, co]).astype(jnp.int32)
    own_half, other_half = pieces
    keep, got = [], []
    for args in (
        ("front", 3, front_block, where, gated, here, own_half[:3]),
        ("back", 5, back_block, where, gated, here, own_half[3:] + other_half),
    ):
        mine, theirs = project(*args)
        kept, given = merge(where, mine, flip(theirs, "co", 1, 2))
        keep.append(kept)
        got.append(flip(given, "zl", 1, 2))
    return finish(where, bucket_of_slot, keep, got)[None]


def solution(mesh):
    mesh = Mesh(mesh.devices.reshape(2, 4, 2, 2, 4), ("zh", "y", "co", "zl", "x"))
    in_specs = (
        P(DP, CTX),
        P(),
        P(DP, None, None),
        P(),
        P(DP, None, None, CTX),
        P(None, None, CTX),
        P(None, CTX),
        P(None, CTX),
        P(CTX),
        P(DP, None, CTX),
    )
    out_specs = P(DP, CTX, None)
    return jax.shard_map(body, mesh=mesh, in_specs=in_specs, out_specs=out_specs, check_vma=False)
```

```python
import functools

import jax
import jax.numpy as jnp
from jax import lax
from jax.experimental import pallas as pl
from jax.experimental.pallas import tpu as pltpu
from jax.sharding import Mesh
from jax.sharding import PartitionSpec as P

F32 = jnp.float32
BF16 = jnp.bfloat16
D = 4096
SEQ = 1024
EPS = 1e-06
OFFSETS = (0, 3, 1, 2)
DP = ("zh", "y", "co")
CTX = ("zl", "x")


def shift(value, axis, step):
    return lax.ppermute(value, axis, [(i, (i + step) % 4) for i in range(4)])


def flip(value, axes, bits, size):
    return lax.ppermute(value, axes, [(i, i ^ bits) for i in range(size)])


def rings(values, axes, after=()):
    near = []
    for value, axis in zip(values, axes):
        near += [shift(value, axis, 1), shift(value, axis, -1)]
    near = lax.optimization_barrier((*near, *after))[:4]
    far = []
    for i, axis in enumerate(axes):
        half = values[i].shape[0] // 2
        far += [shift(near[2 * i][:half], axis, 1), shift(near[2 * i + 1][half:], axis, -1)]
    far = lax.optimization_barrier(tuple(far))
    return [(values[i], *near[2 * i : 2 * i + 2], *far[2 * i : 2 * i + 2]) for i in range(2)]


def filter_kernel(decay, residue, toep):
    for g in range(2):
        time = lax.broadcasted_iota(jnp.int32, (16, SEQ), 1).astype(F32)
        terms = jnp.exp(-decay[:, g : g + 1] * time) * residue[:, g : g + 1]
        filt = jnp.sum(terms, axis=0, keepdims=True).astype(BF16).astype(F32)
        filt = jnp.concatenate([filt, jnp.zeros((1, 128), F32)], axis=1)
        lagged = pltpu.roll(
            jnp.broadcast_to(filt, (128, SEQ + 128)), 0, 1, stride=1, stride_axis=0
        ).astype(BF16)
        for k in range(4):
            toep[g, k, 0:128, :] = lagged[:, 256 * k : 256 * k + 256]
            if k == 0:
                toep[g, k, 128:256, 0:128] = jnp.zeros((128, 128), BF16)
                toep[g, k, 128:256, 128:256] = lagged[:, 0:128]
            else:
                toep[g, k, 128:256, :] = lagged[:, 256 * k - 128 : 256 * k + 128]


def filters(decay, residue):
    vmem = pl.BlockSpec(memory_space=pltpu.VMEM)
    return pl.pallas_call(
        filter_kernel,
        out_shape=jax.ShapeDtypeStruct((2, 4, 256, 256), BF16),
        in_specs=[vmem] * 2,
        out_specs=vmem,
        name="filters",
    )(decay, residue)


def mixer_kernel(recv, taps, skip, toep, out, prod, query):
    table = recv[0, 0:96, :].astype(F32)
    extra = recv[0, 96:112, :].astype(F32)
    square = extra[8:9] + extra[9:10]
    for i in range(1, 8):
        table = table + recv[i, 0:96, :].astype(F32)
        extra = recv[i, 96:112, :].astype(F32)
        square = square + extra[8:9] + extra[9:10]
    table = (table * lax.rsqrt(square / D + EPS)).astype(BF16)

    vocab = lax.broadcasted_iota(jnp.int32, (512, 512), 0).astype(F32)
    lane = lax.broadcasted_iota(jnp.int32, (96, SEQ), 1)

    def one_pair(i, carry):
        extra = recv[i, 96:112, :].astype(F32)
        for j in range(2):
            parts = []
            for a in range(2):
                r = 2 * j + a
                ids = extra[r : r + 1] * 256.0 + extra[4 + r : 5 + r]
                hot = jnp.where(vocab == ids, 1.0, 0.0).astype(BF16)
                parts.append(jnp.dot(table, hot, preferred_element_type=F32))
            z0 = jnp.concatenate(parts, axis=1)
            z1 = jnp.where(lane >= 1, pltpu.roll(z0, 1, 1), 0.0)
            z2 = jnp.where(lane >= 2, pltpu.roll(z0, 2, 1), 0.0)
            f = taps[0] * z0 + taps[1] * z1 + taps[2] * z2
            u = (f[32:64] * f[64:96]).astype(BF16)
            rows = pl.ds(pl.multiple_of((2 * i + j) * 16, 16), 16)
            for g in range(2):
                for b in range(4):
                    cols = slice(256 * b, 256 * b + 256)
                    prod[g, b, rows, :] = u[16 * g : 16 * g + 16, cols]
                    query[g, b, rows, :] = f[16 * g : 16 * g + 16, cols]
        return carry

    lax.fori_loop(0, 8, one_pair, 0, unroll=4)

    for g in range(2):
        for b in range(4):
            mixed = skip[g] * prod[g, b].astype(F32)
            for a in range(b + 1):
                mixed = mixed + jnp.dot(prod[g, a], toep[g, b - a], preferred_element_type=F32)
            gated = (query[g, b] * mixed).astype(BF16)
            for n in range(16):
                for h in range(2):
                    c = 2 * b + h
                    lanes = 256 * (n % 2) + 128 * (c // 4)
                    out[c % 4, n // 2, 16 * g : 16 * g + 16, lanes : lanes + 128] = gated[
                        16 * n : 16 * n + 16, 128 * h : 128 * h + 128
                    ]


def mixer(recv, taps, skip, toep):
    vmem = pl.BlockSpec(memory_space=pltpu.VMEM)
    return pl.pallas_call(
        mixer_kernel,
        out_shape=jax.ShapeDtypeStruct((4, 8, 32, 512), BF16),
        in_specs=[vmem] * 4,
        out_specs=vmem,
        scratch_shapes=[
            pltpu.VMEM((2, 4, 256, 256), BF16),
            pltpu.VMEM((2, 4, 256, 256), F32),
        ],
        compiler_params=pltpu.CompilerParams(vmem_limit_bytes=32 << 20),
        cost_estimate=pl.CostEstimate(
            flops=2 * 16 * 96 * 512 * 1024, bytes_accessed=4 << 20, transcendentals=0
        ),
        name="mixer",
    )(recv, taps, skip, toep)


def front_block(refs, i, xr, s):
    return refs[i].at[4 * xr + s]


def back_block(refs, i, xr, s):
    if i == 0:
        return refs[xr // 2].at[4 * (xr % 2) + s]
    at = 4 * (i - 1) + s
    return refs[2 + xr].at[at] if xr < 3 else refs[5 + at // 8].at[at % 8]


def project_kernel(count, block, where, gated, ids, *refs):
    mine, theirs, right, hot = refs[-4:]
    x, zl, co = where[0], where[3], where[4]

    for r in range(4):
        x_of = lax.rem(x + OFFSETS[r], 4)
        right[256 * r : 256 * r + 256, :] = gated[x_of]
        word = lax.broadcasted_iota(jnp.int32, (32, 512), 0) + ((zl * 4 + x_of) * 2 + co) * 32
        hot[32 * r : 32 * r + 32, :] = jnp.where(word == ids[...], 1.0, 0.0).astype(BF16)

    for i in range(count):
        for s in range(4):
            tiles = [block(refs, i, xr, s) for xr in range(4)]
            rows = jnp.concatenate([t[0:128, :] for t in tiles], axis=1)
            words = jnp.concatenate(
                [t[128:144, 128 * h : 128 * h + 128] for t in tiles for h in range(2)], axis=0
            )
            total = jnp.dot(rows, right[...], preferred_element_type=F32)
            total = total + lax.dot_general(
                words, hot[...], (((0,), (0,)), ((), ())), preferred_element_type=F32
            )
            cols = slice(128 * s, 128 * s + 128)
            mine[i, cols, :] = jnp.where(co == 0, total[:, 0:256], total[:, 256:512])
            theirs[i, cols, :] = jnp.where(co == 0, total[:, 256:512], total[:, 0:256]).astype(
                BF16
            )


def project(name, count, block, where, gated, ids, pieces):
    vmem = pl.BlockSpec(memory_space=pltpu.VMEM)
    smem = pl.BlockSpec(memory_space=pltpu.SMEM)
    return pl.pallas_call(
        functools.partial(project_kernel, count, block),
        out_shape=(
            jax.ShapeDtypeStruct((count, 512, 256), F32),
            jax.ShapeDtypeStruct((count, 512, 256), BF16),
        ),
        in_specs=[smem] + [vmem] * (2 + len(pieces)),
        out_specs=(vmem, vmem),
        scratch_shapes=[pltpu.VMEM((1024, 512), BF16), pltpu.VMEM((128, 512), BF16)],
        compiler_params=pltpu.CompilerParams(vmem_limit_bytes=32 << 20),
        cost_estimate=pl.CostEstimate(
            flops=2 * 512 * 512 * count * 1024, bytes_accessed=3 * count << 20, transcendentals=0
        ),
        name=name,
    )(where, gated, ids, *pieces)


def merge_kernel(where, mine, theirs, keep, give):
    zl = where[3]
    for i in range(mine.shape[0]):
        total = mine[i] + theirs[i].astype(F32)
        low, high = total[:, 0:128], total[:, 128:256]
        keep[i] = jnp.where(zl == 0, low, high)
        give[i] = jnp.where(zl == 0, high, low).astype(BF16)


def merge(where, mine, theirs):
    vmem = pl.BlockSpec(memory_space=pltpu.VMEM)
    smem = pl.BlockSpec(memory_space=pltpu.SMEM)
    return pl.pallas_call(
        merge_kernel,
        out_shape=(
            jax.ShapeDtypeStruct((mine.shape[0], 512, 128), F32),
            jax.ShapeDtypeStruct((mine.shape[0], 512, 128), BF16),
        ),
        in_specs=[smem, vmem, vmem],
        out_specs=(vmem, vmem),
        compiler_params=pltpu.CompilerParams(vmem_limit_bytes=16 << 20),
        name="merge",
    )(where, mine, theirs)


def finish_kernel(where, bucket, keep0, keep1, got0, got1, out):
    y, zh = where[1], where[2]
    for p in range(2):
        for r in range(4):
            keep, got, i = (keep0, got0, r) if p == 0 and r < 3 else (keep1, got1, p * (r + 1))
            for s in range(4):
                rows = slice(128 * s, 128 * s + 128)
                total = keep[i, rows, :] + got[i, rows, :].astype(F32)
                slot = 16 * lax.rem(zh + p, 2) + 4 * lax.rem(y + OFFSETS[r], 4) + s
                cols = pl.ds(pl.multiple_of(bucket[slot] * 128, 128), 128)
                out[:, cols] = total.T.astype(BF16)


def finish(where, bucket, keep, got):
    vmem = pl.BlockSpec(memory_space=pltpu.VMEM)
    smem = pl.BlockSpec(memory_space=pltpu.SMEM)
    return pl.pallas_call(
        finish_kernel,
        out_shape=jax.ShapeDtypeStruct((128, D), BF16),
        in_specs=[smem, smem] + [vmem] * 4,
        out_specs=vmem,
        compiler_params=pltpu.CompilerParams(vmem_limit_bytes=24 << 20),
        name="finish",
    )(where, bucket, *keep, *got)


def body(
    token_ids,
    bucket_of_slot,
    embed_tiles,
    norm_gain,
    in_tiles,
    short_taps,
    decay_rate,
    residue,
    skip_gain,
    out_tiles,
):
    zh, y, co, zl, x = (lax.axis_index(a) for a in ("zh", "y", "co", "zl", "x"))
    zy = zh * 4 + y
    c = zl * 4 + x
    d = zy * 2 + co

    core_index = lax.broadcasted_iota(jnp.int32, (2, 8, 128), 0)
    ctx_index = lax.broadcasted_iota(jnp.int32, (2, 8, 128), 1)
    ids = jnp.where((core_index == co) & (ctx_index == c), token_ids[None], 0)
    ids = ids + shift(ids, "x", 1) + shift(ids, "x", -1) + shift(ids, "x", 2)
    ids, in_tiles = lax.optimization_barrier((ids, in_tiles))
    ids = ids + sum(flip(ids, ("co", "zl"), b, 4) for b in (1, 2, 3))
    here = lax.dynamic_index_in_dim(ids.reshape(2, 2, 4, 128), x, 2, keepdims=False)
    here = here.reshape(1, 512)
    ids = ids.reshape(4, 512)
    ids_rows = jnp.concatenate([ids // 256, ids % 256]).astype(BF16)

    def tile_for(core):
        rows = lax.dynamic_slice_in_dim(out_tiles, core * 256, 256, axis=2)
        words = lax.dynamic_slice_in_dim(embed_tiles, (c * 2 + core) * 32, 32, axis=1)
        words = words.reshape(2, 2, 16, 128).transpose(0, 2, 1, 3).reshape(2, 16, 256)
        return jnp.concatenate([rows, words], axis=1)

    ours, lent = tile_for(co), tile_for(1 - co)

    def by_core(own, sibling):
        return jnp.concatenate([jnp.where(co == 0, own, sibling), jnp.where(co == 0, sibling, own)])

    tiles = by_core(ours, flip(lent, "co", 1, 2))
    across = by_core(flip(ours, "zh", 1, 2), flip(lent, ("zh", "co"), 3, 4))

    buckets = lax.dynamic_slice_in_dim(bucket_of_slot, 2 * d, 2)
    gain = jnp.take(norm_gain.reshape(32, 128), buckets, axis=0)
    embed_f32 = embed_tiles.astype(F32)
    scaled = (embed_f32 * gain[:, None, :]).astype(BF16)
    square = jnp.sum(embed_f32 * embed_f32, axis=(0, 2))
    high = lax.reduce_precision(square, 8, 7)
    square_rows = jnp.stack([high, square - high]).astype(BF16)

    def partial_for(core):
        weights = lax.dynamic_slice_in_dim(in_tiles, core * 256, 256, axis=3).reshape(2, 128, 768)
        return lax.dot_general(
            weights, scaled, (((0, 1), (0, 2)), ((), ())), preferred_element_type=F32
        )

    given = jnp.concatenate(
        [partial_for(1 - co).astype(BF16), square_rows, jnp.zeros((14, 512), BF16)]
    )
    taken = flip(given, "co", 1, 2).astype(F32)
    table = (partial_for(co) + taken[:768]).astype(BF16).reshape(3, 8, 32, 512)
    square = square + taken[768] + taken[769]
    high = lax.reduce_precision(square, 8, 7)
    square_rows = jnp.stack([high, square - high]).astype(BF16)
    extra = jnp.concatenate([ids_rows, square_rows, jnp.zeros((6, 512), BF16)])
    packed = jnp.concatenate(
        [table[0], table[1], table[2], jnp.broadcast_to(extra[None], (8, 16, 512))], axis=1
    )
    parts = rings((tiles, across), ("x", "y"), (packed,))
    parts = [jnp.concatenate(blocks) for blocks in parts]
    pieces = rings(parts, ("y", "x"))

    packed = lax.all_to_all(packed, ("zh", "y"), split_axis=0, concat_axis=0, tiled=True)

    first = co * 256 + zy * 32
    taps = lax.dynamic_slice_in_dim(short_taps, first, 32, axis=2).reshape(3, 96, 1)
    skip = lax.dynamic_slice_in_dim(skip_gain, first, 32).reshape(2, 1, 16)
    skip = jnp.broadcast_to(skip, (2, 16, 16)).reshape(2, 256, 1)
    decay = lax.dynamic_slice_in_dim(decay_rate, co * 16 + zy * 2, 2, axis=1)
    weight = lax.dynamic_slice_in_dim(residue, co * 16 + zy * 2, 2, axis=1)
    gated = mixer(packed, taps, skip, filters(decay, weight))
    gated = lax.all_to_all(
        gated.reshape(32, 32, 512), ("x", "zh", "y"), split_axis=0, concat_axis=0, tiled=True
    ).reshape(4, 256, 512)

    where = jnp.stack([x, y, zh, zl, co]).astype(jnp.int32)
    own_half, other_half = pieces
    keep, got = [], []
    for args in (
        ("front", 3, front_block, where, gated, here, own_half[:3]),
        ("back", 5, back_block, where, gated, here, own_half[3:] + other_half),
    ):
        mine, theirs = project(*args)
        kept, given = merge(where, mine, flip(theirs, "co", 1, 2))
        keep.append(kept)
        got.append(flip(given, "zl", 1, 2))
    return finish(where, bucket_of_slot, keep, got)[None]


def solution(mesh):
    mesh = Mesh(mesh.devices.reshape(2, 4, 2, 2, 4), ("zh", "y", "co", "zl", "x"))
    in_specs = (
        P(DP, CTX),
        P(),
        P(DP, None, None),
        P(),
        P(DP, None, None, CTX),
        P(None, None, CTX),
        P(None, CTX),
        P(None, CTX),
        P(CTX),
        P(DP, None, CTX),
    )
    out_specs = P(DP, CTX, None)
    return jax.shard_map(body, mesh=mesh, in_specs=in_specs, out_specs=out_specs, check_vma=False)
```
